32 devices in a mesh: dp: 2 (over y), expert: 16 (over z, x, core).
Axes of the slice: x: 2, y: 2, z: 4, core: 2. Of those that a mesh axis runs over, the one named last changes fastest.
Arguments:
- tokens: bfloat16 [256, 4096], P(('dp', 'expert')), may hold values from -6 to 6
- expert_ids: int32 [256, 8], P(('dp', 'expert')), may hold values from 0 to 15, all different within a row; in each aligned block of 8 rows (0 to 7, 8 to 15, ...) at most 6 rows name the same one
- gate_values: float32 [256, 8], P(('dp', 'expert')), may hold values from 0.05 to 1
- w_gate: bfloat16 [16, 4096, 2048], P('expert', None, 'dp'), may hold values from -0.09375 to 0.09375
- w_up: bfloat16 [16, 4096, 2048], P('expert', None, 'dp'), may hold values from -0.09375 to 0.09375
- w_down: bfloat16 [16, 2048, 4096], P('expert', 'dp'), may hold values from -0.125 to 0.125
- s_gate: bfloat16 [4096, 2048], P(None, 'dp'), may hold values from -0.09375 to 0.09375
- s_up: bfloat16 [4096, 2048], P(None, 'dp'), may hold values from -0.09375 to 0.09375
- s_down: bfloat16 [2048, 4096], P('dp'), may hold values from -0.125 to 0.125
Outputs:
- mixed: bfloat16 [256, 4096], P(('dp', 'expert'))
The draws below stay inside these ranges and needn't reach their ends.
Inputs may be any that keep to these rules, and one draw needn't show every extreme that they name: `expert_ids`: each row names 8 different experts; the 8 rows of one device name one expert at most 6 times.
All inputs are finite; a program needn't handle non-finite values.
Results may differ from the reference program's by a relative error of at most 0.0054.
Values may be sent and summed in bfloat16 or wider, within the bound.
A program may use at most 128 MiB of HBM per device.

```python
import math
import jax
import jax.numpy as jnp
import numpy as np
from jax import lax

D = 4096
FF = 2048
SFF = 2048
TOP = 8
TOK_DEV = 8
EXPERTS = 16
TOKENS = 256
CAP = 6
N_DP = 2


def steps_of(key, shape, shards, least, top_value):
    def one(dim, shards_of):
        draws = jax.random.uniform(jax.random.fold_in(jax.random.fold_in(key, 6), dim), (shards_of,), jnp.float32, least / len(shards), top_value / len(shards))
        return jnp.repeat(jnp.exp(draws), shape[dim] // shards_of).reshape((-1,) + (1,) * (len(shape) - dim - 1))

    level = one(*shards[0])
    for cut in shards[1:]:
        level = level * one(*cut)
    return level


def deal_out(key, own, number, rows, number_of, top, reach, skew):
    ranking = jax.random.permutation(key, number_of)
    packed, common = load_shares(number_of, rows * top, reach, skew, True), load_shares(number_of, rows * top, reach, skew, False)
    places = jnp.arange(number_of)

    def named(sizes, turn):
        used = int((sizes > 0).sum())
        fixed = max(1, used // 4)
        moved = fixed + (places - fixed + turn * (used - fixed)) % max(1, number_of - fixed)
        return jnp.zeros((number_of,), jnp.int32).at[ranking[jnp.where(places < fixed, places, moved)]].set(jnp.asarray(sizes, jnp.int32))

    sizes = jnp.where(number % 4 == 0, named(packed, number // 4), named(common, number - number // 4 - 1))
    mixed = jax.random.permutation(jax.random.fold_in(own, 3), number_of)
    source_of, sink = mixed[0:number_of // 2 * 2:2], mixed[1:number_of // 2 * 2:2]
    margin = jnp.minimum(sizes[source_of] - 1, reach - sizes[sink]) // 2
    margin = jnp.where((source_of == ranking[0]) | (sink == ranking[0]) | (sizes[sink] == 0), 0, jnp.maximum(margin, 0))
    moved = jax.random.randint(jax.random.fold_in(own, 4), (number_of // 2,), 0, 1 << 20) % (margin + 1)
    sizes = sizes.at[source_of].add(-moved).at[sink].add(moved)
    members = jnp.searchsorted(jnp.cumsum(sizes), jnp.arange(rows * top), side="right").astype(jnp.int32)
    listing = members.reshape(top, rows).T
    listing = listing[jax.random.permutation(jax.random.fold_in(own, 1), rows)]
    turn = jax.random.randint(jax.random.fold_in(own, 2), (rows, 1), 0, top)
    return jnp.take_along_axis(listing, (jnp.arange(top)[None, :] + turn) % top, axis=1)


def load_shares(amount, total, most, slope, full):
    weights = [(1 << 20) // math.isqrt(grade ** slope) + 1 for grade in range(1, amount + 1)]
    largest = most if full else min(most, max(-(-total // amount), total * weights[0] // sum(weights)))
    least = 1 if total - largest >= amount - 1 else 0
    counts, spare = [largest] + [least] * (amount - 1), total - largest - least * (amount - 1)
    while spare > 0:
        movable = [i for i in range(1, amount) if counts[i] < largest] or [i for i in range(1, amount) if counts[i] < most]
        whole, left = sum([weights[i] for i in movable]), spare
        for i in movable:
            more = min(most - counts[i], max(1, left * weights[i] // whole), spare)
            counts[i] = counts[i] + more
            spare = spare - more
    return np.array(counts)


def gaussian(rng, shape, scale, limit, shards=(), kind=jnp.bfloat16):
    factor_of = steps_of(rng, shape, shards, -0.22, 0.18) if shards else 1.0
    drawn = jax.random.normal(rng, shape, jnp.float32) * scale * factor_of
    return jnp.minimum(jnp.maximum(drawn, -limit), limit).astype(kind)


def setup_inputs(seed: int = 0) -> dict:
    key_of = jax.random.split(jax.random.key(seed), 10)
    tokens = gaussian(key_of[0], (TOKENS, D), 1.0, 6.0, ((0, 32),))
    expert_ids_keys = jax.random.split(jax.random.fold_in(key_of[1], 1), TOKENS // TOK_DEV)
    expert_ids_turns = jax.random.permutation(jax.random.fold_in(key_of[1], 3), TOKENS // TOK_DEV)
    expert_ids = jax.vmap(lambda own, number: deal_out(jax.random.fold_in(key_of[1], 2), own, number, TOK_DEV, EXPERTS, TOP, CAP, 2))(expert_ids_keys, expert_ids_turns).reshape((TOKENS, TOP))
    gate_values = jnp.clip(jnp.exp(math.log(1.0) - 2.9957323 * jax.random.uniform(key_of[2], (TOKENS, TOP), jnp.float32) ** steps_of(key_of[2], (TOKENS, TOP), ((0, 32),), -0.2, 0.2)), 0.05, 1.0)
    w_gate = gaussian(key_of[3], (EXPERTS, D, FF), D ** -0.5, 0.09375, ((0, 16), (2, 2)))
    w_up = gaussian(key_of[4], (EXPERTS, D, FF), D ** -0.5, 0.09375, ((0, 16), (2, 2)))
    w_down = gaussian(key_of[5], (EXPERTS, FF, D), FF ** -0.5, 0.125, ((0, 16), (1, 2)))
    s_gate = gaussian(key_of[6], (D, SFF), D ** -0.5, 0.09375, ((1, 2),))
    s_up = gaussian(key_of[7], (D, SFF), D ** -0.5, 0.09375, ((1, 2),))
    s_down = gaussian(key_of[8], (SFF, D), SFF ** -0.5, 0.125, ((0, 2),))
    return {"tokens": tokens, "expert_ids": expert_ids, "gate_values": gate_values, "w_gate": w_gate, "w_up": w_up, "w_down": w_down, "s_gate": s_gate, "s_up": s_up, "s_down": s_down}


def swiglu(rows, gate_w, up_w, down_w):
    gate = jnp.dot(rows, gate_w, preferred_element_type=jnp.float32)
    up = jnp.dot(rows, up_w, preferred_element_type=jnp.float32)
    hidden = (jax.nn.silu(gate) * up).astype(jnp.bfloat16)
    return jnp.dot(hidden, down_w, preferred_element_type=jnp.float32)


def expert_block_sum(rows, gate_w, up_w, down_w):
    gate = jnp.dot(rows, gate_w, preferred_element_type=jnp.float32)
    up = jnp.dot(rows, up_w, preferred_element_type=jnp.float32)
    hidden = (jax.nn.silu(gate) * up).astype(jnp.bfloat16)
    share = FF // N_DP
    blocks = hidden.reshape(rows.shape[0], N_DP, share).astype(jnp.float32)
    downs = down_w.reshape(N_DP, share, D).astype(jnp.float32)
    total = jnp.zeros((rows.shape[0], D), jnp.float32)
    for block in range(N_DP):
        part = jnp.dot(blocks[:, block, :], downs[block], precision=lax.Precision.HIGHEST, preferred_element_type=jnp.float32)
        rounded = lax.optimization_barrier(part.astype(jnp.bfloat16))
        total = total + rounded.astype(jnp.float32)
    return total


def reference(tokens, expert_ids, gate_values, w_gate, w_up, w_down, s_gate, s_up, s_down):
    total = swiglu(tokens, s_gate, s_up, s_down)
    bound = (TOKENS // TOK_DEV) * CAP

    def one_expert(carry, index):
        hits = expert_ids == index
        weight = jnp.sum(jnp.where(hits, gate_values, jnp.float32(0.0)), axis=1)
        chosen = jnp.any(hits, axis=1)
        count = jnp.sum(chosen.astype(jnp.int32)).astype(jnp.int32)
        picked = jnp.nonzero(chosen, size=bound, fill_value=0)[0].astype(jnp.int32)
        outputs = expert_block_sum(tokens[picked], w_gate[index], w_up[index], w_down[index])
        live = jnp.arange(bound, dtype=jnp.int32) < count
        scale = jnp.where(live, weight[picked], jnp.float32(0.0))
        return carry.at[picked].add(scale[:, None] * outputs), None

    indices = jnp.arange(EXPERTS, dtype=jnp.int32)
    total, unused = lax.scan(one_expert, total, indices)
    return total.astype(jnp.bfloat16)
```

```python
import functools

import jax
import jax.numpy as jnp
from jax import lax
from jax.experimental import pallas as pl
from jax.experimental.pallas import tpu as pltpu
from jax.sharding import PartitionSpec as P

LANES = 128
BF16 = jnp.bfloat16
F32 = jnp.float32


def swiglu(rows, gate_w, up_w, down_w):
    gate = jnp.dot(rows, gate_w, preferred_element_type=jnp.float32)
    up = jnp.dot(rows, up_w, preferred_element_type=jnp.float32)
    hidden = (jax.nn.silu(gate) * up).astype(jnp.bfloat16)
    return jnp.dot(hidden, down_w, preferred_element_type=jnp.float32)


def slot_tables(route_ids, route_gates, experts, capacity):
    row_count, picks = route_ids.shape
    listed = route_ids.reshape(-1)
    expert_range = jnp.arange(experts, dtype=jnp.int32)
    marks = (listed[:, None] == expert_range[None, :]).astype(jnp.int32)
    step = jnp.arange(listed.shape[0], dtype=jnp.int32)
    before = (step[None, :] < step[:, None]).astype(jnp.bfloat16)
    earlier = jnp.dot(before, marks.astype(jnp.bfloat16), preferred_element_type=jnp.float32).astype(jnp.int32)
    position = jnp.sum(earlier * marks, axis=1)
    slot_index = (listed * capacity + position).reshape(row_count, picks)
    slot_range = jnp.arange(experts * capacity, dtype=jnp.int32)
    matches = slot_index[:, :, None] == slot_range[None, None, :]
    picker = jnp.any(matches, axis=1).astype(jnp.bfloat16)
    combiner = jnp.sum(jnp.where(matches, route_gates[:, :, None], jnp.float32(0.0)), axis=1)
    return (picker, combiner)


def dispatch_rows(picker, source_rows):
    placed = jnp.einsum("rs,rd->sd", picker, source_rows, preferred_element_type=jnp.float32)
    return placed.astype(jnp.bfloat16)


def exchange_layer(tokens, expert_ids, gate_values, w_gate, w_up, w_down, s_gate, s_up, s_down):
    experts = lax.axis_size("expert")
    groups = lax.axis_size("dp")
    own_rows, width = tokens.shape
    picks = expert_ids.shape[1]
    capacity = max(2, min(own_rows, 3 * own_rows * picks // (2 * experts)))
    gate_local = w_gate[0]
    up_local = w_up[0]
    down_local = w_down[0]
    column = lax.all_gather(tokens, "dp", axis=0, tiled=True)
    column_ids, column_gates = (
        lax.all_gather(expert_ids, "dp", axis=0, tiled=True),
        lax.all_gather(gate_values, "dp", axis=0, tiled=True),
    )
    column_cap = capacity * groups
    picker, combiner = slot_tables(column_ids, column_gates, experts, column_cap)
    outgoing = dispatch_rows(picker, column).reshape(experts, column_cap, width)
    arrived = lax.all_to_all(outgoing, "expert", split_axis=0, concat_axis=0, tiled=True)
    items = arrived.shape[1]
    partial_value = swiglu(
        arrived.reshape(experts * items, width), gate_local, up_local, down_local
    )
    partial_value = partial_value.astype(jnp.bfloat16).reshape(experts, items, width)
    returned = lax.all_to_all(partial_value, "expert", split_axis=0, concat_axis=0, tiled=True)
    returned_rows = returned.reshape(experts * column_cap, width)
    routed = jnp.dot(
        combiner,
        returned_rows.astype(jnp.float32),
        precision=lax.Precision.HIGHEST,
        preferred_element_type=jnp.float32,
    )
    mixed = lax.psum_scatter(
        swiglu(column, s_gate, s_up, s_down) + routed, "dp", scatter_dimension=0, tiled=True
    )
    return mixed.astype(jnp.bfloat16)


HERE, Y_NEXT, X_NEXT, ACROSS = 3, 2, 1, 0
DOWN_PARTS = 4
TILE = 256


def fused_kernel(depth_z, token_ref, ids_ref, gates_ref, wg_hbm, wu_hbm, wd_hbm, sg_hbm, su_hbm, sd_hbm, out_ref,
                 blocks, rows, wg, wu, wd, sgu, sd, hidden, shared, coef_ref, kept, core_out, core_in, flat_out, flat_in,
                 side_out, side_in, line_out, line_in, load_sem, gsend, grecv, csend, crecv, asend, arecv, bsend, brecv,
                 lsend, lrecv):
    own, width = token_ref.shape
    experts = lax.axis_size("expert")
    place = lax.axis_index("expert")
    group = lax.axis_index("dp")
    core = lax.rem(place, 2)
    across_x = lax.rem(lax.div(place, 2), 2)
    other_core = {"dp": group, "expert": place + 1 - 2 * core}
    x_next = {"dp": group, "expert": place + 2 - 4 * across_x}
    y_next = {"dp": 1 - group, "expert": place}

    def along_z(steps):
        return {"dp": group, "expert": lax.rem(place + 4 * steps, experts)}

    loads = []

    def load(src, dst):
        copy = pltpu.make_async_copy(src, dst, load_sem.at[len(loads)])
        copy.start()
        loads.append(copy)

    piece = sd.shape[0]
    sharers = experts * piece // sg_hbm.shape[1]
    first = pl.multiple_of(lax.div(place, sharers) * piece, piece)
    load(sg_hbm.at[:, pl.ds(first, piece)], sgu.at[:, pl.ds(0, piece)])
    load(su_hbm.at[:, pl.ds(first, piece)], sgu.at[:, pl.ds(piece, piece)])
    inner = wg.shape[1]
    for at in range(0, inner, TILE):
        load(wg_hbm.at[0, :, pl.ds(at, TILE)], wg.at[:, pl.ds(at, TILE)])
        load(wu_hbm.at[0, :, pl.ds(at, TILE)], wu.at[:, pl.ds(at, TILE)])
    load(sd_hbm.at[pl.ds(first, piece), :], sd)
    part = width // DOWN_PARTS
    for n in range(DOWN_PARTS):
        load(wd_hbm.at[0, :, pl.ds(n * part, part)], wd.at[:, pl.ds(n * part, part)])

    def slot(own_core, column, turn):
        return (own_core * 4 + column) * depth_z + turn

    mine = slot(1, HERE, 0)
    blocks[mine, :, pl.ds(0, width)] = token_ref[...]
    lane = lax.broadcasted_iota(jnp.int32, (own, LANES), 1)
    expert_of = lax.rem(lane, experts)
    term_of = lax.div(lane, experts)
    gate = jnp.zeros((own, LANES), F32)
    for k in range(ids_ref.shape[1]):
        gate = gate + jnp.where(ids_ref[:, k:k + 1] == expert_of, gates_ref[:, k:k + 1], 0.0)
    high = gate.astype(BF16).astype(F32)
    middle = (gate - high).astype(BF16).astype(F32)
    low = gate - high - middle
    terms = jnp.where(term_of == 0, high, jnp.where(term_of == 1, middle, jnp.where(term_of == 2, low, 0.0)))
    blocks[mine, :, pl.ds(width, LANES)] = terms.astype(BF16)

    barrier = pltpu.get_barrier_semaphore()
    peers = [other_core, x_next, y_next] + [along_z(k) for k in range(1, depth_z)]
    for peer in peers:
        pl.semaphore_signal(barrier, inc=1, device_id=peer, device_id_type=pl.DeviceIdType.MESH)
    pl.semaphore_wait(barrier, len(peers))

    started = []

    def push(src, dst, send, recv, peer):
        copy = pltpu.make_async_remote_copy(src_ref=src, dst_ref=dst, send_sem=send, recv_sem=recv, device_id=peer,
                                            device_id_type=pl.DeviceIdType.MESH)
        copy.start()
        started.append(copy)

    gathers = [0]

    def pass_on(here, there, peer):
        push(blocks.at[here], blocks.at[there], gsend.at[gathers[0]], grecv.at[there], peer)
        gathers[0] += 1

    def arrived(at):
        pltpu.make_async_copy(blocks.at[at], blocks.at[at], grecv.at[at]).wait()

    def to_core(column, turn):
        pass_on(slot(1, column, turn), slot(0, column, turn), other_core)

    def to_x(column, turn):
        pass_on(slot(1, column, turn), slot(1, column ^ 2, turn), x_next)

    def to_y(column, turn):
        pass_on(slot(1, column, turn), slot(1, column ^ 1, turn), y_next)

    half = depth_z // 2
    order = [0]
    for k in range(1, half + 1):
        order += [k] if 2 * k == depth_z else [k, depth_z - k]

    def spread(turn):
        if turn:
            arrived(slot(1, HERE, turn))
        to_x(HERE, turn)
        to_y(HERE, turn)
        if turn == 0:
            for k in order[1:]:
                pass_on(mine, slot(1, HERE, depth_z - k), along_z(k))
        to_core(HERE, turn)

    def relay(turn):
        arrived(slot(1, X_NEXT, turn))
        if turn < half:
            to_y(X_NEXT, turn)
        to_core(X_NEXT, turn)
        arrived(slot(1, Y_NEXT, turn))
        if turn >= half:
            to_x(Y_NEXT, turn)
        to_core(Y_NEXT, turn)

    spread(order[0])
    for before, turn in zip(order, order[1:]):
        spread(turn)
        relay(before)
    relay(order[-1])
    for turn in order:
        arrived(slot(1, ACROSS, turn))
        to_core(ACROSS, turn)
    for turn in order:
        for column in (HERE, X_NEXT, Y_NEXT, ACROSS):
            arrived(slot(0, column, turn))

    def pack(i, carry):
        pair = [blocks[2 * i + j, :, pl.ds(0, width)].astype(F32) for j in range(2)]
        tail = [blocks[2 * i + j, :, pl.ds(width, LANES)].astype(F32) for j in range(2)]
        at = pl.ds(pl.multiple_of(i * 2 * own, 2 * own), 2 * own)
        rows[at, :] = jnp.concatenate(pair, axis=0).astype(BF16)
        lanes = lax.broadcasted_iota(jnp.int32, (2 * own, LANES), 1)
        ours = (lax.rem(lanes, experts) == place) & (lanes < 3 * experts)
        coef_ref[at, :] = jnp.sum(jnp.where(ours, jnp.concatenate(tail, axis=0), 0.0), axis=1, keepdims=True)
        return carry

    total = rows.shape[0]
    lax.fori_loop(0, total // (2 * own), pack, 0)

    for copy in loads[:2]:
        copy.wait()
    both = jnp.dot(rows[...], sgu[...], preferred_element_type=F32)
    value = jax.nn.silu(both[:, :piece]) * both[:, piece:]
    share_of = lax.div(lax.broadcasted_iota(jnp.int32, (total, piece), 1), piece // sharers)
    shared[...] = jnp.where(share_of == lax.rem(place, sharers), value, 0.0).astype(BF16)

    for i in range(inner // TILE):
        loads[2 + 2 * i].wait()
        loads[3 + 2 * i].wait()

    def hidden_tile(j, carry):
        at = pl.ds(pl.multiple_of(j * TILE, TILE), TILE)
        gated = jnp.dot(rows[...], wg[:, at], preferred_element_type=F32)
        up = jnp.dot(rows[...], wu[:, at], preferred_element_type=F32)
        hidden[:, at] = (jax.nn.silu(gated) * up).astype(BF16)
        return carry

    lax.fori_loop(0, inner // TILE, hidden_tile, 0)
    for copy in loads[2 + 2 * (inner // TILE):]:
        copy.wait()

    split = total // 2
    column_rows = depth_z * own
    cut = half * own

    def down(n):
        def tile(j, carry):
            src = pl.ds(pl.multiple_of(n * part + j * TILE, TILE), TILE)
            dst = pl.ds(pl.multiple_of(j * TILE, TILE), TILE)
            routed = jnp.dot(hidden[...], wd[:, src], preferred_element_type=F32)
            common = jnp.dot(shared[...], sd[:, src], preferred_element_type=F32)
            value = routed * coef_ref[...] + common
            core_out[n, :, dst] = value[:split].astype(BF16)
            kept[n, :, dst] = value[split:]
            return carry

        lax.fori_loop(0, part // TILE, tile, 0)
        push(core_out.at[n], core_in.at[n], csend.at[n], crecv.at[n], other_core)

    def landed(ref, sem):
        pltpu.make_async_copy(ref, ref, sem).wait()

    def flat(n):
        landed(core_in.at[n], crecv.at[n])
        at = pl.ds(0, column_rows)
        flat_out[n, :, :] = (kept[n, at, :] + core_in[n, at, :].astype(F32)).astype(BF16)
        push(flat_out.at[n, pl.ds(0, cut)], flat_in.at[n, pl.ds(0, cut)], asend.at[2 * n], arecv.at[2 * n], y_next)
        push(flat_out.at[n, pl.ds(cut, column_rows - cut)], flat_in.at[n, pl.ds(cut, column_rows - cut)],
             asend.at[2 * n + 1], arecv.at[2 * n + 1], x_next)

    def side(n):
        at = pl.ds(column_rows, 2 * column_rows)
        summed = kept[n, at, :] + core_in[n, at, :].astype(F32)
        landed(flat_in.at[n, pl.ds(0, cut)], arecv.at[2 * n])
        landed(flat_in.at[n, pl.ds(cut, column_rows - cut)], arecv.at[2 * n + 1])
        came = flat_in[n].astype(F32)
        side_out[n, 0] = jnp.concatenate([summed[:cut] + came[:cut], summed[cut:column_rows]], axis=0).astype(BF16)
        side_out[n, 1] = jnp.concatenate(
            [summed[column_rows:column_rows + cut], summed[column_rows + cut:] + came[cut:]], axis=0).astype(BF16)
        push(side_out.at[n, 0], side_in.at[n, 0], bsend.at[2 * n], brecv.at[2 * n], x_next)
        push(side_out.at[n, 1], side_in.at[n, 1], bsend.at[2 * n + 1], brecv.at[2 * n + 1], y_next)

    def line(n):
        at = pl.ds(3 * column_rows, column_rows)
        summed = kept[n, at, :] + core_in[n, at, :].astype(F32)
        landed(side_in.at[n, 0], brecv.at[2 * n])
        landed(side_in.at[n, 1], brecv.at[2 * n + 1])
        summed = summed + side_in[n, 0].astype(F32) + side_in[n, 1].astype(F32)
        kept[n, pl.ds(0, own), :] = summed[:own]
        for k in order[1:]:
            line_out[n, k] = summed[k * own:(k + 1) * own].astype(BF16)
            push(line_out.at[n, k], line_in.at[n, depth_z - k], lsend.at[n * depth_z + k],
                 lrecv.at[n * depth_z + depth_z - k], along_z(k))

    def finish(n):
        result = kept[n, pl.ds(0, own), :]
        for k in order[1:]:
            landed(line_in.at[n, k], lrecv.at[n * depth_z + k])
            result = result + line_in[n, k].astype(F32)
        out_ref[:, pl.ds(n * part, part)] = result.astype(out_ref.dtype)

    stages = (down, flat, side, line, finish)
    for step in range(DOWN_PARTS + len(stages) - 1):
        for lag, stage in enumerate(stages):
            if 0 <= step - lag < DOWN_PARTS:
                stage(step - lag)
    for copy in started:
        copy.wait_send()


def fused_bytes(tokens, w_gate, devices):
    own, width = tokens.shape
    inner = w_gate.shape[2]
    total = own * devices
    weights = 2 * (3 * width * inner + 3 * width * LANES)
    gathered = 2 * total * (3 * (width + LANES))
    return weights + gathered + 10 * total * width + 4 * total * LANES


def fused_layer(tokens, expert_ids, gate_values, w_gate, w_up, w_down, s_gate, s_up, s_down):
    experts = lax.axis_size("expert")
    devices = experts * lax.axis_size("dp")
    depth_z = experts // 4
    own, width = tokens.shape
    inner = w_gate.shape[2]
    total = own * devices
    part = width // DOWN_PARTS
    split = total // 2
    column_rows = depth_z * own
    sends = 16 // 4 * depth_z + 3 * depth_z * 4
    dma = pltpu.SemaphoreType.DMA
    scratch = [
        pltpu.VMEM((devices, own, width + LANES), BF16),
        pltpu.VMEM((total, width), BF16),
        pltpu.VMEM((width, inner), BF16),
        pltpu.VMEM((width, inner), BF16),
        pltpu.VMEM((inner, width), BF16),
        pltpu.VMEM((width, 2 * LANES), BF16),
        pltpu.VMEM((LANES, width), BF16),
        pltpu.VMEM((total, inner), BF16),
        pltpu.VMEM((total, LANES), BF16),
        pltpu.VMEM((total, 1), F32),
        pltpu.VMEM((DOWN_PARTS, split, part), F32),
        pltpu.VMEM((DOWN_PARTS, split, part), BF16),
        pltpu.VMEM((DOWN_PARTS, split, part), BF16),
        pltpu.VMEM((DOWN_PARTS, column_rows, part), BF16),
        pltpu.VMEM((DOWN_PARTS, column_rows, part), BF16),
        pltpu.VMEM((DOWN_PARTS, 2, column_rows, part), BF16),
        pltpu.VMEM((DOWN_PARTS, 2, column_rows, part), BF16),
        pltpu.VMEM((DOWN_PARTS, depth_z, own, part), BF16),
        pltpu.VMEM((DOWN_PARTS, depth_z, own, part), BF16),
        dma((3 + 2 * (inner // TILE) + DOWN_PARTS,)),
        dma((sends,)),
        dma((devices,)),
        dma((DOWN_PARTS,)),
        dma((DOWN_PARTS,)),
        dma((2 * DOWN_PARTS,)),
        dma((2 * DOWN_PARTS,)),
        dma((2 * DOWN_PARTS,)),
        dma((2 * DOWN_PARTS,)),
        dma((depth_z * DOWN_PARTS,)),
        dma((depth_z * DOWN_PARTS,)),
    ]
    vmem = pl.BlockSpec(memory_space=pltpu.VMEM)
    hbm = pl.BlockSpec(memory_space=pl.ANY)
    return pl.pallas_call(
        functools.partial(fused_kernel, depth_z),
        out_shape=jax.ShapeDtypeStruct((own, width), BF16),
        in_specs=[vmem] * 3 + [hbm] * 6,
        out_specs=vmem,
        scratch_shapes=scratch,
        compiler_params=pltpu.CompilerParams(collective_id=0, has_side_effects=True,
                                             vmem_limit_bytes=VMEM_BYTES),
        cost_estimate=pl.CostEstimate(flops=6 * total * width * (inner + LANES),
                                      bytes_accessed=6 * width * (inner + LANES), transcendentals=total * inner),
    )(tokens, expert_ids, gate_values, w_gate, w_up, w_down, s_gate, s_up, s_down)


VMEM_BYTES = 60 * 2**20


def per_device(tokens, expert_ids, gate_values, w_gate, w_up, w_down, s_gate, s_up, s_down):
    experts = lax.axis_size("expert")
    groups = lax.axis_size("dp")
    own, width = tokens.shape
    args = (tokens, expert_ids, gate_values, w_gate, w_up, w_down, s_gate, s_up, s_down)
    inner = w_gate.shape[2]
    pieces = s_gate.shape[1] // LANES
    fits = (
        groups == 2
        and experts % 8 == 0
        and 3 * experts <= LANES
        and own % 8 == 0
        and width % (DOWN_PARTS * TILE) == 0
        and inner % TILE == 0
        and s_gate.shape[1] % LANES == 0
        and experts % pieces == 0
        and fused_bytes(tokens, w_gate, groups * experts) <= VMEM_BYTES
    )
    return fused_layer(*args) if fits else exchange_layer(*args)


def solution(mesh):
    placed = (
        P(("dp", "expert"), None),
        P(("dp", "expert"), None),
        P(("dp", "expert"), None),
        P("expert", None, "dp"),
        P("expert", None, "dp"),
        P("expert", "dp", None),
        P(None, "dp"),
        P(None, "dp"),
        P("dp", None),
    )
    return jax.shard_map(
        per_device, mesh=mesh, in_specs=placed, out_specs=P(("dp", "expert"), None), check_vma=False
    )
```
